32 devices in a mesh: group: 2 (over x), slab: 16 (over z, y, core).
Axes of the slice: x: 2, y: 2, z: 4, core: 2. Of those that a mesh axis runs over, the one named last changes fastest.
Arguments:
- green: bfloat16 [2, 16, 2, 256, 256], P('group', 'slab'), parts along dimension 0
- couplings: bfloat16 [16, 2, 256, 256], P('slab')
- gamma: float32 [16, 256], P('slab'), may hold values from 0.01 to 0.1
- occupation: float32 [2, 16], P('group', 'slab'), parts along dimension 0, may hold values from 0 to 1
- lead_occ: float32 [2], P('group'), parts along dimension 0, may hold values from 0.5 to 1.5
- energy_weight: float32 [2], P('group'), parts along dimension 0, may hold values from 0.5 to 2
Outputs:
- left_lesser: float32 [2, 16, 2, 256, 256], P('group', 'slab'), parts along dimension 0
- currents: float32 [32], P(('group', 'slab')), parts along dimension 0
The draws below stay inside these ranges and needn't reach their ends.
There are 2 independent parts, one for each index of `group`. The reference program is written for one: setup_inputs(seed, part) draws one part's arguments, and reference() takes and returns one part's arrays. A program takes and returns all parts, laid end to end along the dimension named above; an argument that names none is the same for every part. Nothing has to cross between parts.
All inputs are finite; a program needn't handle non-finite values.
Results may differ from the reference program's by a relative error of at most 0.0003.
Values sent between devices are 32-bit elements; how exact they have to be, the bound alone decides.
A program may use at most 256 MiB of HBM per device.

```python
import math
import jax
import jax.numpy as jnp
from jax import lax

NORB = 256
ENERGIES = 1
SLABS = 16


def diagonal_heavy(key, lead_shape, magnitude, spread):
    key_off, key_phase = jax.random.split(key)
    full_shape = lead_shape + (2, NORB, NORB)
    off = jax.random.normal(key_off, full_shape, jnp.float32)
    off = off * (spread / math.sqrt(NORB))
    phase = jax.random.uniform(key_phase, lead_shape + (NORB,), jnp.float32, -math.pi, math.pi)
    diag = jnp.stack([magnitude * jnp.cos(phase), magnitude * jnp.sin(phase)], axis=-2)
    eye = jnp.eye(NORB, dtype=jnp.float32)
    return off + diag[..., :, None] * eye


def draw_green(key, part):
    key = jax.random.fold_in(key, 11)
    key_rate, key_rest = jax.random.split(key)
    lead_shape = (ENERGIES, SLABS)
    rate = jnp.exp(jax.random.uniform(key_rate, lead_shape + (NORB,), jnp.float32, math.log(0.3), math.log(60.0)))
    magnitude = jnp.exp(-rate / SLABS)
    return diagonal_heavy(key_rest, lead_shape, magnitude, 0.22).astype(jnp.bfloat16)


def draw_couplings(key, part):
    key = jax.random.fold_in(key, 23)
    magnitude = jnp.ones((SLABS, NORB), jnp.float32)
    return diagonal_heavy(key, (SLABS,), magnitude, 0.22).astype(jnp.bfloat16)


def block_levels(stream_key, extent, shards, low, largest):
    level, own = 1.0, jax.random.fold_in(stream_key, 6)
    for axis_at, blocks in shards:
        steps = jnp.exp(jax.random.uniform(jax.random.fold_in(own, axis_at), (blocks,), jnp.float32, low / len(shards), largest / len(shards)))
        level = level * jnp.repeat(steps, extent[axis_at] // blocks).reshape([-1 if axis == axis_at else 1 for axis in range(len(extent))])
    return level


def setup_inputs(seed: int = 0, part: int = 0) -> dict:
    splits = jax.random.split(jax.random.key(seed), 7)
    part_splits = jax.random.split(jax.random.fold_in(splits[6], part), 7)
    green = draw_green(jax.random.fold_in(jax.random.fold_in(splits[6], part), 71), part)
    couplings = draw_couplings(jax.random.fold_in(splits[6], 71), part)
    gamma = jnp.clip(jnp.exp(math.log(0.1) - 2.3025851 * jax.random.uniform(splits[2], (SLABS, NORB), jnp.float32) ** block_levels(splits[2], (SLABS, NORB), ((0, 16),), -0.2, 0.2)), 0.01, 0.1)
    occupation = jnp.clip(1.0 * jax.random.uniform(part_splits[3], (ENERGIES, SLABS), jnp.float32) ** block_levels(part_splits[3], (ENERGIES, SLABS), ((1, 16),), -0.2, 0.2), 0.0, 1.0)
    lead_occ = jnp.clip(jax.random.uniform(part_splits[4], (ENERGIES,), jnp.float32, 0.5, 1.5), 0.5, 1.5)
    energy_weight = jnp.clip(jnp.exp(jax.random.uniform(part_splits[5], (ENERGIES,), jnp.float32, math.log(0.5), math.log(2.0))), 0.5, 2.0)
    return dict(green=green, couplings=couplings, gamma=gamma, occupation=occupation, lead_occ=lead_occ, energy_weight=energy_weight)


def mult(left, right):
    return jnp.dot(left, right, preferred_element_type=jnp.float32, precision=lax.Precision.HIGHEST)


def cdot(left, right):
    real_part = mult(left[0], right[0]) - mult(left[1], right[1])
    imag_part = mult(left[0], right[1]) + mult(left[1], right[0])
    return jnp.stack([real_part, imag_part])


def herm(block):
    return jnp.stack([block[0].T, -block[1].T])


def imtrace(left, right):
    return jnp.sum(left[0] * right[1].T + left[1] * right[0].T)


def reference(green, couplings, gamma, occupation, lead_occ, energy_weight):
    eye = jnp.eye(NORB, dtype=jnp.float32)
    zeros = jnp.zeros((NORB, NORB), jnp.float32)
    total = jnp.zeros((SLABS,), jnp.float32)
    lessers = []
    for energy in range(ENERGIES):
        def source_of(block, gam, occ):
            full = block.astype(jnp.float32)
            return occ * cdot(full * gam[None, None, :], herm(full))

        def forward(state, items):
            block, coupling, gam, occ = items
            amap = cdot(block, coupling)
            product = cdot(amap, state)
            flow = imtrace(product, herm(coupling.astype(jnp.float32)))
            fresh = cdot(product, herm(amap)) + source_of(block, gam, occ)
            return fresh, (fresh, flow)

        start = jnp.stack([lead_occ[energy] * eye, zeros])
        items = (green[energy], couplings, gamma, occupation[energy])
        _, (states, flows) = lax.scan(forward, start, items)

        def backward(state, items):
            block, coupling, gam, occ = items
            full = block.astype(jnp.float32)
            cfull = coupling.astype(jnp.float32)
            back = imtrace(full, state)
            inner = cdot(cdot(full, state), herm(full)) + source_of(block, gam, occ)
            return cdot(cdot(herm(cfull), inner), cfull), back

        _, backs = lax.scan(backward, jnp.stack([zeros, zeros]), items, reverse=True)
        total = total + energy_weight[energy] * (flows - backs) / NORB
        lessers.append(states)
    return jnp.stack(lessers), total
```

```python
import jax
import jax.numpy as jnp
from jax import lax
from jax.experimental import pallas as pl
from jax.experimental.pallas import tpu as pltpu
from jax.sharding import PartitionSpec as P

F32 = jnp.float32
BF16 = jnp.bfloat16
CHUNKS = 2


def split(value):
    high = value.astype(BF16)
    return high, (value - high.astype(F32)).astype(BF16)


def dot(left, right):
    return jnp.dot(left, right, preferred_element_type=F32)


def kernel(
    green,
    coupling,
    gamma,
    occupation,
    lead_occ,
    energy_weight,
    out,
    current,
    maps,
    sources,
    their_map,
    their_source,
    w_high,
    w_low,
    q_high,
    q_low,
    r_high,
    r_low,
    uv,
    total_source,
    chain_in,
    chain_out,
    mid_in,
    mid_out,
    trace_w,
    sums,
    swap_send,
    swap_recv,
    chain_send,
    chain_recv,
    mid_send,
    mid_recv,
):
    n = green.shape[-1]
    rows = n // CHUNKS
    count = lax.axis_size("slab")
    index = lax.axis_index("slab")
    core = lax.rem(index, 2)
    chip = lax.div(index, 2)
    chips = count // 2
    partner = index + 1 - 2 * core
    ahead = index + 2 - 4 * core
    place = chip + core * (chips - 1 - 2 * chip)
    last = chips - 1

    barrier = pltpu.get_barrier_semaphore()
    pl.semaphore_signal(barrier, inc=1, device_id={"slab": partner})

    @pl.when(chip > 0)
    def _():
        pl.semaphore_signal(barrier, inc=1, device_id={"slab": index - 2})

    @pl.when(chip < last)
    def _():
        pl.semaphore_signal(barrier, inc=1, device_id={"slab": index + 2})

    def prepare(slot, real, imag, exact=False):
        for part, w_ref, q_ref in ((0, w_high, q_high), (1, w_low, q_low)):
            if exact and part == 1:
                break
            a = split(real)[part]
            b = split(imag)[part]
            w_ref[slot, :n, :n] = a
            w_ref[slot, :n, n:] = b
            w_ref[slot, n:, :n] = b
            w_ref[slot, n:, n:] = -a
            q_ref[slot, :n] = a.astype(F32).T.astype(BF16)
            q_ref[slot, n:] = b.astype(F32).T.astype(BF16)

    def load(ref, chunk):
        at = slice(chunk * rows, (chunk + 1) * rows)
        high, low = split(ref[at, :])
        r_high[at, :] = high
        r_low[at, :] = low
        high, low = split(ref[at, :].T)
        r_high[n:, at] = high
        r_low[n:, at] = low

    def first(slot, exact=False):
        value = dot(w_high[slot], r_high[...]) + dot(w_high[slot], r_low[...])
        if not exact:
            value += dot(w_low[slot], r_high[...])
        uv[...] = value

    def second(slot, chunk, exact=False):
        total = None
        for side in range(2):
            at = slice(side * n + chunk * rows, side * n + (chunk + 1) * rows)
            high, low = split(uv[at, :])
            k = slice(side * n, (side + 1) * n)
            value = dot(high, q_high[slot, k]) + dot(low, q_high[slot, k])
            if not exact:
                value += dot(high, q_low[slot, k])
            total = value if total is None else total + value
        return total

    def chunk_rows(chunk):
        return slice(chunk * rows, (chunk + 1) * rows)

    def swap(which, source, target):
        return pltpu.make_async_remote_copy(
            src_ref=source,
            dst_ref=target,
            send_sem=swap_send.at[which],
            recv_sem=swap_recv.at[which],
            device_id={"slab": partner},
        )

    def chain_copy(chunk):
        return pltpu.make_async_remote_copy(
            src_ref=chain_out.at[pl.ds(chunk * rows, rows)],
            dst_ref=chain_in.at[pl.ds(chunk * rows, rows)],
            send_sem=chain_send.at[chunk],
            recv_sem=chain_recv.at[chunk],
            device_id={"slab": ahead},
        )

    def mid_copy(chunk):
        return pltpu.make_async_remote_copy(
            src_ref=mid_out.at[pl.ds(chunk * rows, rows)],
            dst_ref=mid_in.at[pl.ds(chunk * rows, rows)],
            send_sem=mid_send.at[chunk],
            recv_sem=mid_recv.at[chunk],
            device_id={"slab": partner},
        )

    g_r, g_i = green[0], green[1]
    c_r, c_i = coupling[0], coupling[1]
    maps[0, 0] = dot(g_r, c_r) - dot(g_i, c_i)
    maps[0, 1] = dot(g_r, c_i) + dot(g_i, c_r)
    ct_r = c_r.astype(F32).T.astype(BF16)
    ct_i = c_i.astype(F32).T.astype(BF16)
    maps[1, 0] = dot(ct_r, g_r) + dot(ct_i, g_i)
    maps[1, 1] = dot(ct_r, g_i) - dot(ct_i, g_r)

    pl.semaphore_wait(
        barrier, 1 + (chip > 0).astype(jnp.int32) + (chip < last).astype(jnp.int32)
    )
    swap_map = swap(0, maps.at[1 - core], their_map)
    swap_map.start()

    occ = occupation[0, 0]
    gamma_row = gamma[...] * occ
    f_r, f_i = g_r.astype(F32), g_i.astype(F32)
    uv[:n] = (f_r + f_i) * gamma_row
    uv[n:] = (f_i - f_r) * gamma_row
    q_high[3, :n] = f_r.T.astype(BF16)
    q_high[3, n:] = f_i.T.astype(BF16)
    for chunk in range(CHUNKS):
        sources[0, chunk_rows(chunk), :] = second(3, chunk, exact=True)
    trace_w[...] = 0.5 * ((f_i - f_r) + (f_i + f_r).T)
    prepare(3, ct_r.astype(F32), -ct_i.astype(F32), exact=True)
    for chunk in range(CHUNKS):
        load(sources.at[0], chunk)
    first(3, exact=True)
    for chunk in range(CHUNKS):
        sources[1, chunk_rows(chunk), :] = second(3, chunk, exact=True)
    swap_source = swap(1, sources.at[1 - core], their_source)
    swap_source.start()

    prepare(0, maps[core, 0], maps[core, 1])
    prepare(1, maps[1 - core, 0], maps[1 - core, 1])

    for chunk in range(CHUNKS):
        load(sources.at[core], chunk)
    swap_map.wait_recv()
    prepare(3, their_map[0], their_map[1])
    first(3)
    for chunk in range(CHUNKS):
        total_source[chunk_rows(chunk), :] = second(3, chunk)
    r_high[:n], r_low[:n] = split(maps[core, 0])
    r_high[n:], r_low[n:] = split(-maps[core, 1])
    uv[:n] = (
        dot(w_high[3, :n], r_high[...])
        + dot(w_high[3, :n], r_low[...])
        + dot(w_low[3, :n], r_high[...])
    )
    r_high[:n], r_low[:n] = split(maps[core, 1])
    r_high[n:], r_low[n:] = split(maps[core, 0])
    uv[n:] = (
        dot(w_high[3, :n], r_high[...])
        + dot(w_high[3, :n], r_low[...])
        + dot(w_low[3, :n], r_high[...])
    )
    prepare(2, uv[:n], uv[n:])
    swap_source.wait_recv()
    total_source[...] += their_source[...]

    def flow():
        weight_u = 0.5 * (coupling[0].astype(F32) - coupling[1].astype(F32))
        weight_v = 0.5 * (coupling[0].astype(F32) + coupling[1].astype(F32))
        sums[0] = jnp.sum(uv[:n] * weight_u + uv[n:] * weight_v)

    def back(ref):
        sums[1] = jnp.sum(ref[...] * trace_w[...])

    def emit(ref):
        block = ref[...]
        turned = block.T
        out[0] = 0.5 * (block + turned)
        out[1] = 0.5 * (block - turned)

    def chain():
        @pl.when(place == 0)
        def _():
            row = lax.broadcasted_iota(jnp.int32, (n, n), 0)
            column = lax.broadcasted_iota(jnp.int32, (n, n), 1)
            level = lead_occ[0] * (1 - core).astype(F32)
            chain_in[...] = jnp.where(row == column, level, 0.0)

        for chunk in range(CHUNKS):
            @pl.when(place > 0)
            def _():
                chain_copy(chunk).wait_recv()

            load(chain_in, chunk)

        @pl.when(place < last)
        def _():
            first(2)
            for chunk in range(CHUNKS):
                at = chunk_rows(chunk)
                chain_out[at, :] = second(2, chunk) + total_source[at, :]
                chain_copy(chunk).start()

        first(0)
        for chunk in range(CHUNKS):
            at = chunk_rows(chunk)
            mid_out[at, :] = second(0, chunk) + sources[core, at, :]
            mid_copy(chunk).start()

        @pl.when(core == 0)
        def _():
            flow()
            emit(mid_out)

        @pl.when(core == 1)
        def _():
            back(chain_in)

    def middle():
        for chunk in range(CHUNKS):
            mid_copy(chunk).wait_recv()

        @pl.when(core == 0)
        def _():
            back(mid_in)

        @pl.when(core == 1)
        def _():
            for chunk in range(CHUNKS):
                load(mid_in, chunk)
            first(1)
            for chunk in range(CHUNKS):
                at = chunk_rows(chunk)
                chain_spare[at, :] = second(1, chunk) + sources[0, at, :]
            flow()
            emit(chain_spare)

    chain_spare = their_source
    early = (place <= chips // 2).astype(jnp.int32)

    def phase(step, carry):
        @pl.when(step + early == 1)
        def _():
            chain()

        @pl.when(step + early != 1)
        def _():
            middle()

        return carry

    lax.fori_loop(0, 2, phase, 0)
    current[0] = energy_weight[0] * (sums[0] - sums[1]) / n

    swap_map.wait_send()
    swap_source.wait_send()
    for chunk in range(CHUNKS):
        mid_copy(chunk).wait_send()

        @pl.when(place < last)
        def _():
            chain_copy(chunk).wait_send()


def on_device(green, couplings, gamma, occupation, lead_occ, energy_weight):
    n = green.shape[-1]
    vmem = pl.BlockSpec(memory_space=pltpu.VMEM)
    smem = pl.BlockSpec(memory_space=pltpu.SMEM)
    block = lambda *lead: pltpu.VMEM((*lead, n, n), F32)
    wide = lambda *shape: pltpu.VMEM(shape, BF16)
    state, current = pl.pallas_call(
        kernel,
        out_shape=(
            jax.ShapeDtypeStruct((2, n, n), F32),
            jax.ShapeDtypeStruct((1,), F32),
        ),
        in_specs=[vmem, vmem, vmem, smem, smem, smem],
        out_specs=(vmem, smem),
        scratch_shapes=[
            block(2, 2),
            block(2),
            block(2),
            block(),
            wide(4, 2 * n, 2 * n),
            wide(4, 2 * n, 2 * n),
            wide(4, 2 * n, n),
            wide(4, 2 * n, n),
            wide(2 * n, n),
            wide(2 * n, n),
            pltpu.VMEM((2 * n, n), F32),
            block(),
            block(),
            block(),
            block(),
            block(),
            block(),
            pltpu.SMEM((2,), F32),
            pltpu.SemaphoreType.DMA((2,)),
            pltpu.SemaphoreType.DMA((2,)),
            pltpu.SemaphoreType.DMA((CHUNKS,)),
            pltpu.SemaphoreType.DMA((CHUNKS,)),
            pltpu.SemaphoreType.DMA((CHUNKS,)),
            pltpu.SemaphoreType.DMA((CHUNKS,)),
        ],
        compiler_params=pltpu.CompilerParams(
            collective_id=0, has_side_effects=True, vmem_limit_bytes=40 * 2**20
        ),
    )(
        green.reshape(2, n, n),
        couplings.reshape(2, n, n),
        gamma,
        occupation,
        lead_occ,
        energy_weight,
    )
    return state.reshape(1, 1, 2, n, n), current


def solution(mesh):
    return jax.shard_map(
        on_device,
        mesh=mesh,
        in_specs=(
            P("group", "slab", None, None, None),
            P("slab", None, None, None),
            P("slab", None),
            P("group", "slab"),
            P("group"),
            P("group"),
        ),
        out_specs=(P("group", "slab", None, None, None), P(("group", "slab"))),
        check_vma=False,
    )
```

```python
import jax
import jax.numpy as jnp
from jax import lax
from jax.experimental import pallas as pl
from jax.experimental.pallas import tpu as pltpu
from jax.sharding import PartitionSpec as P

F32 = jnp.float32
BF16 = jnp.bfloat16
CHUNKS = 2


def split(value):
    high = value.astype(BF16)
    return high, (value - high.astype(F32)).astype(BF16)


def dot(left, right):
    return jnp.dot(left, right, preferred_element_type=F32)


def kernel(
    green_in,
    coupling_in,
    gamma_in,
    occupation,
    lead_occ,
    energy_weight,
    out,
    current,
    green,
    coupling,
    gamma,
    fetched,
    maps,
    sources,
    their_map,
    their_source,
    w_high,
    w_low,
    q_high,
    q_low,
    r_high,
    r_low,
    uv,
    pair_map,
    pair_source,
    head_out,
    head_map,
    head_source,
    quad_source,
    state_in,
    chain_in,
    chain_out,
    mid_in,
    mid_out,
    trace_w,
    sums,
    swap_send,
    swap_recv,
    head_send,
    head_recv,
    chain_send,
    chain_recv,
    mid_send,
    mid_recv,
):
    n = green.shape[-1]
    rows = n // CHUNKS
    count = lax.axis_size("slab")
    index = lax.axis_index("slab")
    core = lax.rem(index, 2)
    chip = lax.div(index, 2)
    chips = count // 2
    quads = count // 4
    sign = 1 - 2 * core
    partner = index + sign
    next_near = index + 2 * sign
    next_far = index + 4 * sign
    tail = lax.rem(chip + core, 2)
    quad = lax.div(chip, 2)
    place = quad + core * (quads - 1 - 2 * quad)
    last = quads - 1

    fetches = [
        pltpu.make_async_copy(source, target, fetched.at[at])
        for at, (source, target) in enumerate(
            ((green_in, green), (coupling_in, coupling), (gamma_in, gamma))
        )
    ]
    for fetch in fetches:
        fetch.start()

    barrier = pltpu.get_barrier_semaphore()
    pl.semaphore_signal(barrier, inc=1, device_id={"slab": partner})
    greeted = 1
    for step in (-4, -2, 2, 4):
        there = index + step
        inside = jnp.logical_and(there >= 0, there < count)
        greeted = greeted + inside.astype(jnp.int32)

        @pl.when(inside)
        def _():
            pl.semaphore_signal(barrier, inc=1, device_id={"slab": there})

    for fetch in fetches:
        fetch.wait()

    def prepare(slot, real, imag, exact=False):
        for part, w_ref, q_ref in ((0, w_high, q_high), (1, w_low, q_low)):
            if exact and part == 1:
                break
            a = split(real)[part]
            b = split(imag)[part]
            w_ref[slot, :n, :n] = a
            w_ref[slot, :n, n:] = b
            w_ref[slot, n:, :n] = b
            w_ref[slot, n:, n:] = -a
            q_ref[slot, :n] = a.astype(F32).T.astype(BF16)
            q_ref[slot, n:] = b.astype(F32).T.astype(BF16)

    def load(ref, chunk):
        at = slice(chunk * rows, (chunk + 1) * rows)
        high, low = split(ref[at, :])
        r_high[at, :] = high
        r_low[at, :] = low
        high, low = split(ref[at, :].T)
        r_high[n:, at] = high
        r_low[n:, at] = low

    def first(slot, exact=False):
        value = dot(w_high[slot], r_high[...]) + dot(w_high[slot], r_low[...])
        if not exact:
            value += dot(w_low[slot], r_high[...])
        uv[...] = value

    def second(slot, chunk, exact=False):
        total = None
        for side in range(2):
            at = slice(side * n + chunk * rows, side * n + (chunk + 1) * rows)
            high, low = split(uv[at, :])
            k = slice(side * n, (side + 1) * n)
            value = dot(high, q_high[slot, k]) + dot(low, q_high[slot, k])
            if not exact:
                value += dot(high, q_low[slot, k])
            total = value if total is None else total + value
        return total

    def chunk_rows(chunk):
        return slice(chunk * rows, (chunk + 1) * rows)

    def swap(which, source, target):
        return pltpu.make_async_remote_copy(
            src_ref=source,
            dst_ref=target,
            send_sem=swap_send.at[which],
            recv_sem=swap_recv.at[which],
            device_id={"slab": partner},
        )

    def chain_copy(chunk, which):
        return pltpu.make_async_remote_copy(
            src_ref=chain_out.at[pl.ds(chunk * rows, rows)],
            dst_ref=chain_in.at[pl.ds(chunk * rows, rows)],
            send_sem=chain_send.at[which, chunk],
            recv_sem=chain_recv.at[chunk],
            device_id={"slab": (next_far, next_near)[which]},
        )

    def head_copy(which, source, target):
        return pltpu.make_async_remote_copy(
            src_ref=source,
            dst_ref=target,
            send_sem=head_send.at[which],
            recv_sem=head_recv.at[which],
            device_id={"slab": next_near},
        )

    def mid_copy(chunk):
        return pltpu.make_async_remote_copy(
            src_ref=mid_out.at[pl.ds(chunk * rows, rows)],
            dst_ref=mid_in.at[pl.ds(chunk * rows, rows)],
            send_sem=mid_send.at[chunk],
            recv_sem=mid_recv.at[chunk],
            device_id={"slab": partner},
        )

    g_r, g_i = green[0], green[1]
    c_r, c_i = coupling[0], coupling[1]
    maps[0, 0] = dot(g_r, c_r) - dot(g_i, c_i)
    maps[0, 1] = dot(g_r, c_i) + dot(g_i, c_r)
    ct_r = c_r.astype(F32).T.astype(BF16)
    ct_i = c_i.astype(F32).T.astype(BF16)
    maps[1, 0] = dot(ct_r, g_r) + dot(ct_i, g_i)
    maps[1, 1] = dot(ct_r, g_i) - dot(ct_i, g_r)

    pl.semaphore_wait(barrier, greeted)
    swap_map = swap(0, maps.at[1 - core], their_map)
    swap_map.start()

    occ = occupation[0, 0]
    gamma_row = gamma[...] * occ
    f_r, f_i = g_r.astype(F32), g_i.astype(F32)
    uv[:n] = (f_r + f_i) * gamma_row
    uv[n:] = (f_i - f_r) * gamma_row
    q_high[3, :n] = f_r.T.astype(BF16)
    q_high[3, n:] = f_i.T.astype(BF16)
    for chunk in range(CHUNKS):
        sources[0, chunk_rows(chunk), :] = second(3, chunk, exact=True)
    trace_w[...] = 0.5 * ((f_i - f_r) + (f_i + f_r).T)
    prepare(3, ct_r.astype(F32), -ct_i.astype(F32), exact=True)
    for chunk in range(CHUNKS):
        load(sources.at[0], chunk)
    first(3, exact=True)
    for chunk in range(CHUNKS):
        sources[1, chunk_rows(chunk), :] = second(3, chunk, exact=True)
    swap_source = swap(1, sources.at[1 - core], their_source)
    swap_source.start()

    def multiply(slot, ref):
        real, imag = split(ref[0]), split(ref[1])
        r_high[:n], r_low[:n] = real
        r_high[n:], r_low[n:] = -imag[0], -imag[1]
        for side in range(2):
            if side == 1:
                r_high[:n], r_low[:n] = imag
                r_high[n:], r_low[n:] = real
            uv[side * n : (side + 1) * n] = (
                dot(w_high[slot, :n], r_high[...])
                + dot(w_high[slot, :n], r_low[...])
                + dot(w_low[slot, :n], r_high[...])
            )

    head_map_copy = head_copy(0, pair_map, head_map)
    head_source_copy = head_copy(1, head_out, head_source)
    sends_map = jnp.logical_and(tail == 0, place > 0)
    swap_map.wait_recv()
    prepare(3, their_map[0], their_map[1])
    own = maps.at[core]
    multiply(3, own)
    pair_map[0] = uv[:n]
    pair_map[1] = uv[n:]

    @pl.when(sends_map)
    def _():
        head_map_copy.start()

    for chunk in range(CHUNKS):
        load(sources.at[core], chunk)
    first(3)
    swap_source.wait_recv()
    for chunk in range(CHUNKS):
        at = chunk_rows(chunk)
        pair_source[at, :] = second(3, chunk) + their_source[at, :]

    @pl.when(sends_map)
    def _():
        head_out[...] = pair_source[...]
        head_source_copy.start()

    @pl.when(jnp.logical_or(tail == 1, place == 0))
    def _():
        prepare(2, pair_map[0], pair_map[1])

    prepare(0, maps[core, 0], maps[core, 1])

    @pl.when(core == 1)
    def _():
        prepare(1, maps[0, 0], maps[0, 1])

    def flow():
        weight_u = 0.5 * (coupling[0].astype(F32) - coupling[1].astype(F32))
        weight_v = 0.5 * (coupling[0].astype(F32) + coupling[1].astype(F32))
        sums[0] = jnp.sum(uv[:n] * weight_u + uv[n:] * weight_v)

    def back(ref):
        sums[1] = jnp.sum(ref[...] * trace_w[...])

    def emit(ref):
        block = ref[...]
        turned = block.T
        out[0] = 0.5 * (block + turned)
        out[1] = 0.5 * (block - turned)

    def relay(slot, source):
        for chunk in range(CHUNKS):
            at = chunk_rows(chunk)
            chain_out[at, :] = second(slot, chunk) + source[at, :]

            @pl.when(place < last)
            def _():
                chain_copy(chunk, 0).start()

        @pl.when(place < last)
        def _():
            for chunk in range(CHUNKS):
                chain_copy(chunk, 1).start()

    def receive():
        for chunk in range(CHUNKS):
            chain_copy(chunk, 0).wait_recv()
            load(chain_in, chunk)

    def chain():
        @pl.when(tail == 0)
        def _():
            @pl.when(place == 0)
            def _():
                row = lax.broadcasted_iota(jnp.int32, (n, n), 0)
                column = lax.broadcasted_iota(jnp.int32, (n, n), 1)
                level = lead_occ[0] * (1 - core).astype(F32)
                chain_in[...] = jnp.where(row == column, level, 0.0)
                for chunk in range(CHUNKS):
                    load(chain_in, chunk)
                first(2)
                for chunk in range(CHUNKS):
                    at = chunk_rows(chunk)
                    head_out[at, :] = second(2, chunk) + pair_source[at, :]
                head_source_copy.start()

            @pl.when(place > 0)
            def _():
                receive()

            state_in[...] = chain_in[...]

        @pl.when(tail == 1)
        def _():
            @pl.when(place > 0)
            def _():
                head_map_copy.wait_recv()
                prepare(3, head_map[0], head_map[1])
                multiply(2, head_map)
                prepare(4, uv[:n], uv[n:])

            head_source_copy.wait_recv()

            @pl.when(jnp.logical_or(place == 0, place < last))
            def _():
                for chunk in range(CHUNKS):
                    load(head_source, chunk)
                first(2)

            @pl.when(place == 0)
            def _():
                relay(2, pair_source)
                state_in[...] = head_source[...]

            @pl.when(place > 0)
            def _():
                @pl.when(place < last)
                def _():
                    for chunk in range(CHUNKS):
                        at = chunk_rows(chunk)
                        quad_source[at, :] = second(2, chunk) + pair_source[at, :]

                receive()

                @pl.when(place < last)
                def _():
                    first(4)
                    relay(4, quad_source)

                first(3)
                for chunk in range(CHUNKS):
                    at = chunk_rows(chunk)
                    state_in[at, :] = second(3, chunk) + head_source[at, :]

            for chunk in range(CHUNKS):
                load(state_in, chunk)

        first(0)
        for chunk in range(CHUNKS):
            at = chunk_rows(chunk)
            mid_out[at, :] = second(0, chunk) + sources[core, at, :]
            mid_copy(chunk).start()

        @pl.when(core == 0)
        def _():
            flow()
            emit(mid_out)

        @pl.when(core == 1)
        def _():
            back(state_in)

    def middle():
        for chunk in range(CHUNKS):
            mid_copy(chunk).wait_recv()

        @pl.when(core == 0)
        def _():
            back(mid_in)

        @pl.when(core == 1)
        def _():
            for chunk in range(CHUNKS):
                load(mid_in, chunk)
            first(1)
            for chunk in range(CHUNKS):
                at = chunk_rows(chunk)
                chain_spare[at, :] = second(1, chunk) + sources[0, at, :]
            flow()
            emit(chain_spare)

    chain_spare = their_source
    early = (place <= quads // 2).astype(jnp.int32)

    def phase(step, carry):
        @pl.when(step + early == 1)
        def _():
            chain()

        @pl.when(step + early != 1)
        def _():
            middle()

        return carry

    lax.fori_loop(0, 2, phase, 0)
    current[0] = energy_weight[0] * (sums[0] - sums[1]) / n

    swap_map.wait_send()
    swap_source.wait_send()
    for chunk in range(CHUNKS):
        mid_copy(chunk).wait_send()

    @pl.when(tail == 0)
    def _():
        head_source_copy.wait_send()

        @pl.when(place > 0)
        def _():
            head_map_copy.wait_send()

    @pl.when(jnp.logical_and(tail == 1, place < last))
    def _():
        for which in range(2):
            for chunk in range(CHUNKS):
                chain_copy(chunk, which).wait_send()


def on_device(green, couplings, gamma, occupation, lead_occ, energy_weight):
    n = green.shape[-1]
    vmem = pl.BlockSpec(memory_space=pltpu.VMEM)
    hbm = pl.BlockSpec(memory_space=pl.ANY)
    smem = pl.BlockSpec(memory_space=pltpu.SMEM)
    block = lambda *lead: pltpu.VMEM((*lead, n, n), F32)
    wide = lambda *shape: pltpu.VMEM(shape, BF16)
    state, current = pl.pallas_call(
        kernel,
        out_shape=(
            jax.ShapeDtypeStruct((2, n, n), F32),
            jax.ShapeDtypeStruct((1,), F32),
        ),
        in_specs=[hbm, hbm, hbm, smem, smem, smem],
        out_specs=(vmem, smem),
        scratch_shapes=[
            wide(2, n, n),
            wide(2, n, n),
            pltpu.VMEM((1, n), F32),
            pltpu.SemaphoreType.DMA((3,)),
            block(2, 2),
            block(2),
            block(2),
            block(),
            wide(5, 2 * n, 2 * n),
            wide(5, 2 * n, 2 * n),
            wide(5, 2 * n, n),
            wide(5, 2 * n, n),
            wide(2 * n, n),
            wide(2 * n, n),
            pltpu.VMEM((2 * n, n), F32),
            block(2),
            block(),
            block(),
            block(2),
            block(),
            block(),
            block(),
            block(),
            block(),
            block(),
            block(),
            block(),
            pltpu.SMEM((2,), F32),
            pltpu.SemaphoreType.DMA((2,)),
            pltpu.SemaphoreType.DMA((2,)),
            pltpu.SemaphoreType.DMA((2,)),
            pltpu.SemaphoreType.DMA((2,)),
            pltpu.SemaphoreType.DMA((2, CHUNKS)),
            pltpu.SemaphoreType.DMA((CHUNKS,)),
            pltpu.SemaphoreType.DMA((CHUNKS,)),
            pltpu.SemaphoreType.DMA((CHUNKS,)),
        ],
        compiler_params=pltpu.CompilerParams(
            collective_id=0, has_side_effects=True, vmem_limit_bytes=40 * 2**20
        ),
    )(
        green.reshape(2, n, n),
        couplings.reshape(2, n, n),
        gamma,
        occupation,
        lead_occ,
        energy_weight,
    )
    return state.reshape(1, 1, 2, n, n), current


def solution(mesh):
    return jax.shard_map(
        on_device,
        mesh=mesh,
        in_specs=(
            P("group", "slab", None, None, None),
            P("slab", None, None, None),
            P("slab", None),
            P("group", "slab"),
            P("group"),
            P("group"),
        ),
        out_specs=(P("group", "slab", None, None, None), P(("group", "slab"))),
        check_vma=False,
    )
```

```python
import jax
import jax.numpy as jnp
from jax import lax
from jax.experimental import pallas as pl
from jax.experimental.pallas import tpu as pltpu
from jax.sharding import PartitionSpec as P

F32 = jnp.float32
BF16 = jnp.bfloat16
CHUNKS = 2


def split(value):
    high = value.astype(BF16)
    return high, (value - high.astype(F32)).astype(BF16)


def dot(left, right):
    return jnp.dot(left, right, preferred_element_type=F32)


def kernel(
    green_in,
    coupling_in,
    gamma_in,
    occupation,
    lead_occ,
    energy_weight,
    out,
    current,
    green,
    coupling,
    gamma,
    fetched,
    maps,
    sources,
    their_map,
    their_source,
    w_high,
    w_low,
    q_high,
    q_low,
    r_high,
    r_low,
    uv,
    pair_map,
    pair_source,
    head_out,
    head_map,
    head_source,
    quad_source,
    state_in,
    chain_in,
    chain_out,
    mid_in,
    mid_out,
    trace_w,
    sums,
    swap_send,
    swap_recv,
    head_send,
    head_recv,
    chain_send,
    chain_recv,
    mid_send,
    mid_recv,
):
    n = green.shape[-1]
    rows = n // CHUNKS
    count = lax.axis_size("slab")
    index = lax.axis_index("slab")
    core = lax.rem(index, 2)
    chip = lax.div(index, 2)
    chips = count // 2
    quads = count // 4
    sign = 1 - 2 * core
    partner = index + sign
    next_near = index + 2 * sign
    next_far = index + 4 * sign
    tail = lax.rem(chip + core, 2)
    quad = lax.div(chip, 2)
    place = quad + core * (quads - 1 - 2 * quad)
    last = quads - 1

    fetches = [
        pltpu.make_async_copy(source, target, fetched.at[at])
        for at, (source, target) in enumerate(
            ((green_in, green), (coupling_in, coupling), (gamma_in, gamma))
        )
    ]
    for fetch in fetches:
        fetch.start()

    barrier = pltpu.get_barrier_semaphore()
    pl.semaphore_signal(barrier, inc=1, device_id={"slab": partner})
    greeted = 1
    for step in (-4, -2, 2, 4):
        there = index + step
        inside = jnp.logical_and(there >= 0, there < count)
        greeted = greeted + inside.astype(jnp.int32)

        @pl.when(inside)
        def _():
            pl.semaphore_signal(barrier, inc=1, device_id={"slab": there})

    for fetch in fetches:
        fetch.wait()

    def prepare(slot, real, imag, exact=False):
        for part, w_ref, q_ref in ((0, w_high, q_high), (1, w_low, q_low)):
            if exact and part == 1:
                break
            a = split(real)[part]
            b = split(imag)[part]
            w_ref[slot, :n, :n] = a
            w_ref[slot, :n, n:] = b
            w_ref[slot, n:, :n] = b
            w_ref[slot, n:, n:] = -a
            q_ref[slot, :n] = a.astype(F32).T.astype(BF16)
            q_ref[slot, n:] = b.astype(F32).T.astype(BF16)

    def load(ref, chunk):
        at = slice(chunk * rows, (chunk + 1) * rows)
        high, low = split(ref[at, :])
        r_high[at, :] = high
        r_low[at, :] = low
        high, low = split(ref[at, :].T)
        r_high[n:, at] = high
        r_low[n:, at] = low

    def first(slot, exact=False):
        value = dot(w_high[slot], r_high[...]) + dot(w_high[slot], r_low[...])
        if not exact:
            value += dot(w_low[slot], r_high[...])
        uv[...] = value

    def second(slot, chunk, exact=False):
        total = None
        for side in range(2):
            at = slice(side * n + chunk * rows, side * n + (chunk + 1) * rows)
            high, low = split(uv[at, :])
            k = slice(side * n, (side + 1) * n)
            value = dot(high, q_high[slot, k]) + dot(low, q_high[slot, k])
            if not exact:
                value += dot(high, q_low[slot, k])
            total = value if total is None else total + value
        return total

    def chunk_rows(chunk):
        return slice(chunk * rows, (chunk + 1) * rows)

    def swap(which, source, target):
        return pltpu.make_async_remote_copy(
            src_ref=source,
            dst_ref=target,
            send_sem=swap_send.at[which],
            recv_sem=swap_recv.at[which],
            device_id={"slab": partner},
        )

    def chain_copy(chunk, which):
        return pltpu.make_async_remote_copy(
            src_ref=chain_out.at[pl.ds(chunk * rows, rows)],
            dst_ref=chain_in.at[pl.ds(chunk * rows, rows)],
            send_sem=chain_send.at[which, chunk],
            recv_sem=chain_recv.at[chunk],
            device_id={"slab": (next_far, next_near)[which]},
        )

    def head_copy(which, source, target):
        return pltpu.make_async_remote_copy(
            src_ref=source,
            dst_ref=target,
            send_sem=head_send.at[which],
            recv_sem=head_recv.at[which],
            device_id={"slab": next_near},
        )

    def mid_copy(chunk):
        return pltpu.make_async_remote_copy(
            src_ref=mid_out.at[pl.ds(chunk * rows, rows)],
            dst_ref=mid_in.at[pl.ds(chunk * rows, rows)],
            send_sem=mid_send.at[chunk],
            recv_sem=mid_recv.at[chunk],
            device_id={"slab": partner},
        )

    g_r, g_i = green[0], green[1]
    c_r, c_i = coupling[0], coupling[1]
    maps[0, 0] = dot(g_r, c_r) - dot(g_i, c_i)
    maps[0, 1] = dot(g_r, c_i) + dot(g_i, c_r)
    ct_r = c_r.astype(F32).T.astype(BF16)
    ct_i = c_i.astype(F32).T.astype(BF16)
    maps[1, 0] = dot(ct_r, g_r) + dot(ct_i, g_i)
    maps[1, 1] = dot(ct_r, g_i) - dot(ct_i, g_r)

    pl.semaphore_wait(barrier, greeted)
    swap_map = swap(0, maps.at[1 - core], their_map)
    swap_map.start()

    occ = occupation[0, 0]
    gamma_row = gamma[...] * occ
    f_r, f_i = g_r.astype(F32), g_i.astype(F32)
    uv[:n] = (f_r + f_i) * gamma_row
    uv[n:] = (f_i - f_r) * gamma_row
    q_high[3, :n] = f_r.T.astype(BF16)
    q_high[3, n:] = f_i.T.astype(BF16)
    for chunk in range(CHUNKS):
        sources[0, chunk_rows(chunk), :] = second(3, chunk, exact=True)
    trace_w[...] = 0.5 * ((f_i - f_r) + (f_i + f_r).T)
    prepare(3, ct_r.astype(F32), -ct_i.astype(F32), exact=True)
    for chunk in range(CHUNKS):
        load(sources.at[0], chunk)
    first(3, exact=True)
    for chunk in range(CHUNKS):
        sources[1, chunk_rows(chunk), :] = second(3, chunk, exact=True)
    swap_source = swap(1, sources.at[1 - core], their_source)
    swap_source.start()

    def multiply(slot, ref):
        real, imag = split(ref[0]), split(ref[1])
        r_high[:n], r_low[:n] = real
        r_high[n:], r_low[n:] = -imag[0], -imag[1]
        for side in range(2):
            if side == 1:
                r_high[:n], r_low[:n] = imag
                r_high[n:], r_low[n:] = real
            uv[side * n : (side + 1) * n] = (
                dot(w_high[slot, :n], r_high[...])
                + dot(w_high[slot, :n], r_low[...])
                + dot(w_low[slot, :n], r_high[...])
            )

    head_map_copy = head_copy(0, pair_map, head_map)
    head_source_copy = head_copy(1, head_out, head_source)
    sends_map = jnp.logical_and(tail == 0, place > 0)
    swap_map.wait_recv()
    prepare(3, their_map[0], their_map[1])
    own = maps.at[core]
    multiply(3, own)
    pair_map[0] = uv[:n]
    pair_map[1] = uv[n:]

    @pl.when(sends_map)
    def _():
        head_map_copy.start()

    for chunk in range(CHUNKS):
        load(sources.at[core], chunk)
    first(3)
    swap_source.wait_recv()
    for chunk in range(CHUNKS):
        at = chunk_rows(chunk)
        pair_source[at, :] = second(3, chunk) + their_source[at, :]

    @pl.when(sends_map)
    def _():
        head_out[...] = pair_source[...]
        head_source_copy.start()

    @pl.when(jnp.logical_or(tail == 1, place == 0))
    def _():
        prepare(2, pair_map[0], pair_map[1])

    prepare(0, maps[core, 0], maps[core, 1])

    @pl.when(core == 1)
    def _():
        prepare(1, maps[0, 0], maps[0, 1])

    def flow():
        weight_u = 0.5 * (coupling[0].astype(F32) - coupling[1].astype(F32))
        weight_v = 0.5 * (coupling[0].astype(F32) + coupling[1].astype(F32))
        sums[0] = jnp.sum(uv[:n] * weight_u + uv[n:] * weight_v)

    def back(ref):
        sums[1] = jnp.sum(ref[...] * trace_w[...])

    def emit(ref):
        block = ref[...]
        turned = block.T
        out[0] = 0.5 * (block + turned)
        out[1] = 0.5 * (block - turned)

    def relay(slot, source):
        for chunk in range(CHUNKS):
            at = chunk_rows(chunk)
            chain_out[at, :] = second(slot, chunk) + source[at, :]

            @pl.when(place < last - 1)
            def _():
                chain_copy(chunk, 0).start()

            @pl.when(place == last - 1)
            def _():
                chain_copy(chunk, 1).start()

        for chunk in range(CHUNKS):
            @pl.when(place < last - 1)
            def _():
                chain_copy(chunk, 1).start()

            @pl.when(place == last - 1)
            def _():
                chain_copy(chunk, 0).start()

    def receive():
        for chunk in range(CHUNKS):
            chain_copy(chunk, 0).wait_recv()
            load(chain_in, chunk)

    ends = jnp.logical_and(tail == 1, jnp.logical_and(place == last, place > 0))
    base = 2 - 2 * ends.astype(jnp.int32)

    def hand_over(slot, source):
        for chunk in range(CHUNKS):
            at = chunk_rows(chunk)
            mid_out[at, :] = second(slot, chunk) + source[at, :]
            mid_copy(chunk).start()

    def chain():
        @pl.when(tail == 0)
        def _():
            @pl.when(place == 0)
            def _():
                row = lax.broadcasted_iota(jnp.int32, (n, n), 0)
                column = lax.broadcasted_iota(jnp.int32, (n, n), 1)
                level = lead_occ[0] * (1 - core).astype(F32)
                chain_in[...] = jnp.where(row == column, level, 0.0)
                uv[:n] = level * (pair_map[0] + pair_map[1])
                uv[n:] = level * (pair_map[1] - pair_map[0])
                for chunk in range(CHUNKS):
                    at = chunk_rows(chunk)
                    head_out[at, :] = second(2, chunk) + pair_source[at, :]
                head_source_copy.start()
                for chunk in range(CHUNKS):
                    load(chain_in, chunk)

            @pl.when(place > 0)
            def _():
                receive()

            state_in[...] = chain_in[...]

        @pl.when(tail == 1)
        def _():
            @pl.when(place > 0)
            def _():
                head_map_copy.wait_recv()
                prepare(3, head_map[0], head_map[1])
                multiply(base, head_map)
                prepare(4, uv[:n], uv[n:])

            head_source_copy.wait_recv()
            for chunk in range(CHUNKS):
                load(head_source, chunk)
            first(base)

            @pl.when(place == 0)
            def _():
                relay(2, pair_source)
                state_in[...] = head_source[...]

            @pl.when(place > 0)
            def _():
                for chunk in range(CHUNKS):
                    at = chunk_rows(chunk)
                    quad_source[at, :] = second(base, chunk) + jnp.where(
                        ends, sources[core, at, :], pair_source[at, :]
                    )
                receive()
                first(4)

                @pl.when(jnp.logical_not(ends))
                def _():
                    relay(4, quad_source)

                @pl.when(ends)
                def _():
                    hand_over(4, quad_source)

                first(3)
                for chunk in range(CHUNKS):
                    at = chunk_rows(chunk)
                    state_in[at, :] = second(3, chunk) + head_source[at, :]

            for chunk in range(CHUNKS):
                load(state_in, chunk)

        first(0)

        @pl.when(jnp.logical_not(ends))
        def _():
            hand_over(0, sources.at[core])

        @pl.when(core == 0)
        def _():
            flow()
            emit(mid_out)

        @pl.when(core == 1)
        def _():
            back(state_in)

    def middle():
        for chunk in range(CHUNKS):
            mid_copy(chunk).wait_recv()

        @pl.when(core == 0)
        def _():
            back(mid_in)

        @pl.when(core == 1)
        def _():
            for chunk in range(CHUNKS):
                load(mid_in, chunk)
            first(1)
            for chunk in range(CHUNKS):
                at = chunk_rows(chunk)
                chain_spare[at, :] = second(1, chunk) + sources[0, at, :]
            flow()
            emit(chain_spare)

    chain_spare = their_source
    early = (place <= quads // 2).astype(jnp.int32)

    def phase(step, carry):
        @pl.when(step + early == 1)
        def _():
            chain()

        @pl.when(step + early != 1)
        def _():
            middle()

        return carry

    lax.fori_loop(0, 2, phase, 0)
    current[0] = energy_weight[0] * (sums[0] - sums[1]) / n

    swap_map.wait_send()
    swap_source.wait_send()
    for chunk in range(CHUNKS):
        mid_copy(chunk).wait_send()

    @pl.when(tail == 0)
    def _():
        head_source_copy.wait_send()

        @pl.when(place > 0)
        def _():
            head_map_copy.wait_send()

    @pl.when(jnp.logical_and(tail == 1, place < last))
    def _():
        for which in range(2):
            for chunk in range(CHUNKS):
                chain_copy(chunk, which).wait_send()


def on_device(green, couplings, gamma, occupation, lead_occ, energy_weight):
    n = green.shape[-1]
    vmem = pl.BlockSpec(memory_space=pltpu.VMEM)
    hbm = pl.BlockSpec(memory_space=pl.ANY)
    smem = pl.BlockSpec(memory_space=pltpu.SMEM)
    block = lambda *lead: pltpu.VMEM((*lead, n, n), F32)
    wide = lambda *shape: pltpu.VMEM(shape, BF16)
    state, current = pl.pallas_call(
        kernel,
        out_shape=(
            jax.ShapeDtypeStruct((2, n, n), F32),
            jax.ShapeDtypeStruct((1,), F32),
        ),
        in_specs=[hbm, hbm, hbm, smem, smem, smem],
        out_specs=(vmem, smem),
        scratch_shapes=[
            wide(2, n, n),
            wide(2, n, n),
            pltpu.VMEM((1, n), F32),
            pltpu.SemaphoreType.DMA((3,)),
            block(2, 2),
            block(2),
            block(2),
            block(),
            wide(5, 2 * n, 2 * n),
            wide(5, 2 * n, 2 * n),
            wide(5, 2 * n, n),
            wide(5, 2 * n, n),
            wide(2 * n, n),
            wide(2 * n, n),
            pltpu.VMEM((2 * n, n), F32),
            block(2),
            block(),
            block(),
            block(2),
            block(),
            block(),
            block(),
            block(),
            block(),
            block(),
            block(),
            block(),
            pltpu.SMEM((2,), F32),
            pltpu.SemaphoreType.DMA((2,)),
            pltpu.SemaphoreType.DMA((2,)),
            pltpu.SemaphoreType.DMA((2,)),
            pltpu.SemaphoreType.DMA((2,)),
            pltpu.SemaphoreType.DMA((2, CHUNKS)),
            pltpu.SemaphoreType.DMA((CHUNKS,)),
            pltpu.SemaphoreType.DMA((CHUNKS,)),
            pltpu.SemaphoreType.DMA((CHUNKS,)),
        ],
        compiler_params=pltpu.CompilerParams(
            collective_id=0, has_side_effects=True, vmem_limit_bytes=62 * 2**20
        ),
    )(
        green.reshape(2, n, n),
        couplings.reshape(2, n, n),
        gamma,
        occupation,
        lead_occ,
        energy_weight,
    )
    return state.reshape(1, 1, 2, n, n), current


def solution(mesh):
    return jax.shard_map(
        on_device,
        mesh=mesh,
        in_specs=(
            P("group", "slab", None, None, None),
            P("slab", None, None, None),
            P("slab", None),
            P("group", "slab"),
            P("group"),
            P("group"),
        ),
        out_specs=(P("group", "slab", None, None, None), P(("group", "slab"))),
        check_vma=False,
    )
```

```python
import jax
import jax.numpy as jnp
from jax import lax
from jax.experimental import pallas as pl
from jax.experimental.pallas import tpu as pltpu
from jax.sharding import PartitionSpec as P

F32 = jnp.float32
BF16 = jnp.bfloat16
CHUNKS = 2


def split(value):
    high = value.astype(BF16)
    return high, (value - high.astype(F32)).astype(BF16)


def dot(left, right):
    return jnp.dot(left, right, preferred_element_type=F32)


def kernel(
    green_in,
    coupling_in,
    gamma_in,
    occupation,
    lead_occ,
    energy_weight,
    out,
    current,
    green,
    coupling,
    gamma,
    fetched,
    maps,
    sources,
    their_map,
    their_source,
    w_high,
    w_low,
    q_high,
    q_low,
    r_high,
    r_low,
    uv,
    pair_map,
    pair_source,
    head_out,
    head_map,
    head_source,
    quad_source,
    state_in,
    chain_in,
    chain_out,
    mid_in,
    mid_out,
    trace_w,
    sums,
    swap_send,
    swap_recv,
    head_send,
    head_recv,
    chain_send,
    chain_recv,
    mid_send,
    mid_recv,
):
    n = green.shape[-1]
    rows = n // CHUNKS
    count = lax.axis_size("slab")
    index = lax.axis_index("slab")
    core = lax.rem(index, 2)
    chip = lax.div(index, 2)
    chips = count // 2
    quads = count // 4
    sign = 1 - 2 * core
    partner = index + sign
    next_near = index + 2 * sign
    next_far = index + 4 * sign
    tail = lax.rem(chip + core, 2)
    quad = lax.div(chip, 2)
    place = quad + core * (quads - 1 - 2 * quad)
    last = quads - 1

    fetches = [
        pltpu.make_async_copy(source, target, fetched.at[at])
        for at, (source, target) in enumerate(
            ((green_in, green), (coupling_in, coupling), (gamma_in, gamma))
        )
    ]
    for fetch in fetches:
        fetch.start()

    barrier = pltpu.get_barrier_semaphore()
    pl.semaphore_signal(barrier, inc=1, device_id={"slab": partner})
    greeted = 1
    for step in (-4, -2, 2, 4):
        there = index + step
        inside = jnp.logical_and(there >= 0, there < count)
        greeted = greeted + inside.astype(jnp.int32)

        @pl.when(inside)
        def _():
            pl.semaphore_signal(barrier, inc=1, device_id={"slab": there})

    for fetch in fetches:
        fetch.wait()

    def prepare(slot, real, imag, exact=False):
        for part, w_ref, q_ref in ((0, w_high, q_high), (1, w_low, q_low)):
            if exact and part == 1:
                break
            a = split(real)[part]
            b = split(imag)[part]
            w_ref[slot, :n, :n] = a
            w_ref[slot, :n, n:] = b
            w_ref[slot, n:, :n] = b
            w_ref[slot, n:, n:] = -a
            q_ref[slot, :n] = a.astype(F32).T.astype(BF16)
            q_ref[slot, n:] = b.astype(F32).T.astype(BF16)

    def load(ref, chunk):
        at = slice(chunk * rows, (chunk + 1) * rows)
        high, low = split(ref[at, :])
        r_high[at, :] = high
        r_low[at, :] = low
        high, low = split(ref[at, :].T)
        r_high[n:, at] = high
        r_low[n:, at] = low

    def first(slot, exact=False):
        value = dot(w_high[slot], r_high[...]) + dot(w_high[slot], r_low[...])
        if not exact:
            value += dot(w_low[slot], r_high[...])
        uv[...] = value

    def second(slot, chunk, exact=False):
        total = None
        for side in range(2):
            at = slice(side * n + chunk * rows, side * n + (chunk + 1) * rows)
            high, low = split(uv[at, :])
            k = slice(side * n, (side + 1) * n)
            value = dot(high, q_high[slot, k]) + dot(low, q_high[slot, k])
            if not exact:
                value += dot(high, q_low[slot, k])
            total = value if total is None else total + value
        return total

    def chunk_rows(chunk):
        return slice(chunk * rows, (chunk + 1) * rows)

    def swap(which, source, target):
        return pltpu.make_async_remote_copy(
            src_ref=source,
            dst_ref=target,
            send_sem=swap_send.at[which],
            recv_sem=swap_recv.at[which],
            device_id={"slab": partner},
        )

    def chain_copy(chunk, which):
        return pltpu.make_async_remote_copy(
            src_ref=chain_out.at[pl.ds(chunk * rows, rows)],
            dst_ref=chain_in.at[pl.ds(chunk * rows, rows)],
            send_sem=chain_send.at[which, chunk],
            recv_sem=chain_recv.at[chunk],
            device_id={"slab": (next_far, next_near)[which]},
        )

    def head_copy(which, source, target):
        return pltpu.make_async_remote_copy(
            src_ref=source,
            dst_ref=target,
            send_sem=head_send.at[which],
            recv_sem=head_recv.at[which],
            device_id={"slab": next_near},
        )

    def mid_copy(chunk):
        return pltpu.make_async_remote_copy(
            src_ref=mid_out.at[pl.ds(chunk * rows, rows)],
            dst_ref=mid_in.at[pl.ds(chunk * rows, rows)],
            send_sem=mid_send.at[chunk],
            recv_sem=mid_recv.at[chunk],
            device_id={"slab": partner},
        )

    g_r, g_i = green[0], green[1]
    c_r, c_i = coupling[0], coupling[1]
    maps[0, 0] = dot(g_r, c_r) - dot(g_i, c_i)
    maps[0, 1] = dot(g_r, c_i) + dot(g_i, c_r)
    ct_r = c_r.astype(F32).T.astype(BF16)
    ct_i = c_i.astype(F32).T.astype(BF16)
    maps[1, 0] = dot(ct_r, g_r) + dot(ct_i, g_i)
    maps[1, 1] = dot(ct_r, g_i) - dot(ct_i, g_r)

    pl.semaphore_wait(barrier, greeted)
    swap_map = swap(0, maps.at[1 - core], their_map)
    swap_map.start()

    gamma_row = gamma[...] * occupation[0, 0]

    def source(which):
        real, imag = (
            (maps[1, 0], maps[1, 1])
            if which
            else (green[0].astype(F32), green[1].astype(F32))
        )
        uv[:n] = (real + imag) * gamma_row
        uv[n:] = (imag - real) * gamma_row
        for part, q_ref in ((0, q_high), (1, q_low))[: 1 + which]:
            q_ref[4, :n] = split(real)[part].astype(F32).T.astype(BF16)
            q_ref[4, n:] = split(imag)[part].astype(F32).T.astype(BF16)
        for chunk in range(CHUNKS):
            sources[which, chunk_rows(chunk), :] = second(4, chunk, exact=not which)

    swap_source = swap(1, sources.at[1 - core], their_source)
    for mine in range(2):
        @pl.when(core == mine)
        def _():
            source(1 - mine)
            swap_source.start()
            source(mine)

    def trace_weights():
        f_r, f_i = green[0].astype(F32), green[1].astype(F32)
        trace_w[...] = 0.5 * ((f_i - f_r) + (f_i + f_r).T)

    def own_maps():
        prepare(0, maps[core, 0], maps[core, 1])

        @pl.when(core == 1)
        def _():
            prepare(1, maps[0, 0], maps[0, 1])

        trace_weights()

    def multiply(slot, ref):
        real, imag = split(ref[0]), split(ref[1])
        r_high[:n], r_low[:n] = real
        r_high[n:], r_low[n:] = -imag[0], -imag[1]
        for side in range(2):
            if side == 1:
                r_high[:n], r_low[:n] = imag
                r_high[n:], r_low[n:] = real
            uv[side * n : (side + 1) * n] = (
                dot(w_high[slot, :n], r_high[...])
                + dot(w_high[slot, :n], r_low[...])
                + dot(w_low[slot, :n], r_high[...])
            )

    head_map_copy = head_copy(0, pair_map, head_map)
    head_source_copy = head_copy(1, head_out, head_source)
    sends_map = jnp.logical_and(tail == 0, place > 0)
    swap_map.wait_recv()
    prepare(3, their_map[0], their_map[1])
    own = maps.at[core]
    multiply(3, own)
    pair_map[0] = uv[:n]
    pair_map[1] = uv[n:]

    @pl.when(sends_map)
    def _():
        head_map_copy.start()

    for chunk in range(CHUNKS):
        load(sources.at[core], chunk)
    first(3)
    swap_source.wait_recv()
    for chunk in range(CHUNKS):
        at = chunk_rows(chunk)
        pair_source[at, :] = second(3, chunk) + their_source[at, :]

    @pl.when(sends_map)
    def _():
        head_out[...] = pair_source[...]
        head_source_copy.start()

    @pl.when(jnp.logical_or(tail == 1, place == 0))
    def _():
        prepare(2, pair_map[0], pair_map[1])

    opens = jnp.logical_and(tail == 0, place == 0)

    @pl.when(jnp.logical_not(opens))
    def _():
        own_maps()

    def flow():
        weight_u = 0.5 * (coupling[0].astype(F32) - coupling[1].astype(F32))
        weight_v = 0.5 * (coupling[0].astype(F32) + coupling[1].astype(F32))
        sums[0] = jnp.sum(uv[:n] * weight_u + uv[n:] * weight_v)

    def back(ref):
        sums[1] = jnp.sum(ref[...] * trace_w[...])

    def emit(ref):
        block = ref[...]
        turned = block.T
        out[0] = 0.5 * (block + turned)
        out[1] = 0.5 * (block - turned)

    def relay(slot, source):
        for chunk in range(CHUNKS):
            at = chunk_rows(chunk)
            chain_out[at, :] = second(slot, chunk) + source[at, :]

            @pl.when(place < last - 1)
            def _():
                chain_copy(chunk, 0).start()

            @pl.when(place == last - 1)
            def _():
                chain_copy(chunk, 1).start()

        for chunk in range(CHUNKS):
            @pl.when(place < last - 1)
            def _():
                chain_copy(chunk, 1).start()

            @pl.when(place == last - 1)
            def _():
                chain_copy(chunk, 0).start()

    def receive():
        for chunk in range(CHUNKS):
            chain_copy(chunk, 0).wait_recv()
            load(chain_in, chunk)

    ends = jnp.logical_and(tail == 1, jnp.logical_and(place == last, place > 0))
    base = 2 - 2 * ends.astype(jnp.int32)

    def hand_over(slot, source):
        for chunk in range(CHUNKS):
            at = chunk_rows(chunk)
            mid_out[at, :] = second(slot, chunk) + source[at, :]
            mid_copy(chunk).start()

    def chain():
        @pl.when(tail == 0)
        def _():
            @pl.when(place == 0)
            def _():
                row = lax.broadcasted_iota(jnp.int32, (n, n), 0)
                column = lax.broadcasted_iota(jnp.int32, (n, n), 1)
                level = lead_occ[0] * (1 - core).astype(F32)
                chain_in[...] = jnp.where(row == column, level, 0.0)
                uv[:n] = level * (pair_map[0] + pair_map[1])
                uv[n:] = level * (pair_map[1] - pair_map[0])
                for chunk in range(CHUNKS):
                    at = chunk_rows(chunk)
                    head_out[at, :] = second(2, chunk) + pair_source[at, :]
                head_source_copy.start()
                own_maps()
                for chunk in range(CHUNKS):
                    load(chain_in, chunk)

            @pl.when(place > 0)
            def _():
                receive()

            state_in[...] = chain_in[...]

        @pl.when(tail == 1)
        def _():
            @pl.when(place > 0)
            def _():
                head_map_copy.wait_recv()
                prepare(3, head_map[0], head_map[1])
                multiply(base, head_map)
                prepare(4, uv[:n], uv[n:])

            head_source_copy.wait_recv()
            for chunk in range(CHUNKS):
                load(head_source, chunk)
            first(base)

            @pl.when(place == 0)
            def _():
                relay(2, pair_source)
                state_in[...] = head_source[...]

            @pl.when(place > 0)
            def _():
                for chunk in range(CHUNKS):
                    at = chunk_rows(chunk)
                    quad_source[at, :] = second(base, chunk) + jnp.where(
                        ends, sources[core, at, :], pair_source[at, :]
                    )
                receive()
                first(4)

                @pl.when(jnp.logical_not(ends))
                def _():
                    relay(4, quad_source)

                @pl.when(ends)
                def _():
                    hand_over(4, quad_source)

                first(3)
                for chunk in range(CHUNKS):
                    at = chunk_rows(chunk)
                    state_in[at, :] = second(3, chunk) + head_source[at, :]

            for chunk in range(CHUNKS):
                load(state_in, chunk)

        @pl.when(jnp.logical_or(core == 0, jnp.logical_not(ends)))
        def _():
            first(0)

        @pl.when(jnp.logical_not(ends))
        def _():
            hand_over(0, sources.at[core])

        @pl.when(core == 0)
        def _():
            flow()
            emit(mid_out)

        @pl.when(core == 1)
        def _():
            back(state_in)

    def middle():
        for chunk in range(CHUNKS):
            mid_copy(chunk).wait_recv()

        @pl.when(core == 0)
        def _():
            back(mid_in)

        @pl.when(core == 1)
        def _():
            for chunk in range(CHUNKS):
                load(mid_in, chunk)
            first(1)
            for chunk in range(CHUNKS):
                at = chunk_rows(chunk)
                chain_spare[at, :] = second(1, chunk) + sources[0, at, :]
            flow()
            emit(chain_spare)

    chain_spare = their_source
    early = (place <= quads // 2).astype(jnp.int32)

    def phase(step, carry):
        @pl.when(step + early == 1)
        def _():
            chain()

        @pl.when(step + early != 1)
        def _():
            middle()

        return carry

    lax.fori_loop(0, 2, phase, 0)
    current[0] = energy_weight[0] * (sums[0] - sums[1]) / n

    swap_map.wait_send()
    swap_source.wait_send()
    for chunk in range(CHUNKS):
        mid_copy(chunk).wait_send()

    @pl.when(tail == 0)
    def _():
        head_source_copy.wait_send()

        @pl.when(place > 0)
        def _():
            head_map_copy.wait_send()

    @pl.when(jnp.logical_and(tail == 1, place < last))
    def _():
        for which in range(2):
            for chunk in range(CHUNKS):
                chain_copy(chunk, which).wait_send()


def on_device(green, couplings, gamma, occupation, lead_occ, energy_weight):
    n = green.shape[-1]
    vmem = pl.BlockSpec(memory_space=pltpu.VMEM)
    hbm = pl.BlockSpec(memory_space=pl.ANY)
    smem = pl.BlockSpec(memory_space=pltpu.SMEM)
    block = lambda *lead: pltpu.VMEM((*lead, n, n), F32)
    wide = lambda *shape: pltpu.VMEM(shape, BF16)
    state, current = pl.pallas_call(
        kernel,
        out_shape=(
            jax.ShapeDtypeStruct((2, n, n), F32),
            jax.ShapeDtypeStruct((1,), F32),
        ),
        in_specs=[hbm, hbm, hbm, smem, smem, smem],
        out_specs=(vmem, smem),
        scratch_shapes=[
            wide(2, n, n),
            wide(2, n, n),
            pltpu.VMEM((1, n), F32),
            pltpu.SemaphoreType.DMA((3,)),
            block(2, 2),
            block(2),
            block(2),
            block(),
            wide(5, 2 * n, 2 * n),
            wide(5, 2 * n, 2 * n),
            wide(5, 2 * n, n),
            wide(5, 2 * n, n),
            wide(2 * n, n),
            wide(2 * n, n),
            pltpu.VMEM((2 * n, n), F32),
            block(2),
            block(),
            block(),
            block(2),
            block(),
            block(),
            block(),
            block(),
            block(),
            block(),
            block(),
            block(),
            pltpu.SMEM((2,), F32),
            pltpu.SemaphoreType.DMA((2,)),
            pltpu.SemaphoreType.DMA((2,)),
            pltpu.SemaphoreType.DMA((2,)),
            pltpu.SemaphoreType.DMA((2,)),
            pltpu.SemaphoreType.DMA((2, CHUNKS)),
            pltpu.SemaphoreType.DMA((CHUNKS,)),
            pltpu.SemaphoreType.DMA((CHUNKS,)),
            pltpu.SemaphoreType.DMA((CHUNKS,)),
        ],
        compiler_params=pltpu.CompilerParams(
            collective_id=0, has_side_effects=True, vmem_limit_bytes=62 * 2**20
        ),
    )(
        green.reshape(2, n, n),
        couplings.reshape(2, n, n),
        gamma,
        occupation,
        lead_occ,
        energy_weight,
    )
    return state.reshape(1, 1, 2, n, n), current


def solution(mesh):
    return jax.shard_map(
        on_device,
        mesh=mesh,
        in_specs=(
            P("group", "slab", None, None, None),
            P("slab", None, None, None),
            P("slab", None),
            P("group", "slab"),
            P("group"),
            P("group"),
        ),
        out_specs=(P("group", "slab", None, None, None), P(("group", "slab"))),
        check_vma=False,
    )
```

```python
import jax
import jax.numpy as jnp
from jax import lax
from jax.experimental import pallas as pl
from jax.experimental.pallas import tpu as pltpu
from jax.sharding import PartitionSpec as P

F32 = jnp.float32
BF16 = jnp.bfloat16
CHUNKS = 2


def split(value):
    high = value.astype(BF16)
    return high, (value - high.astype(F32)).astype(BF16)


def dot(left, right):
    return jnp.dot(left, right, preferred_element_type=F32)


def kernel(
    green_in,
    coupling_in,
    gamma_in,
    occupation,
    lead_occ,
    energy_weight,
    out,
    current,
    green,
    coupling,
    gamma,
    fetched,
    maps,
    sources,
    their_map,
    their_source,
    w_high,
    w_low,
    q_high,
    q_low,
    r_high,
    r_low,
    uv,
    pair_map,
    pair_source,
    head_out,
    head_map,
    head_source,
    quad_source,
    state_in,
    chain_in,
    chain_out,
    mid_in,
    mid_out,
    trace_w,
    sums,
    swap_send,
    swap_recv,
    head_send,
    head_recv,
    chain_send,
    chain_recv,
    mid_send,
    mid_recv,
):
    n = green.shape[-1]
    rows = n // CHUNKS
    count = lax.axis_size("slab")
    index = lax.axis_index("slab")
    core = lax.rem(index, 2)
    chip = lax.div(index, 2)
    chips = count // 2
    quads = count // 4
    sign = 1 - 2 * core
    partner = index + sign
    next_near = index + 2 * sign
    next_far = index + 4 * sign
    tail = lax.rem(chip + core, 2)
    quad = lax.div(chip, 2)
    place = quad + core * (quads - 1 - 2 * quad)
    last = quads - 1

    fetches = [
        pltpu.make_async_copy(source, target, fetched.at[at])
        for at, (source, target) in enumerate(
            ((green_in, green), (coupling_in, coupling), (gamma_in, gamma))
        )
    ]
    for fetch in fetches:
        fetch.start()

    barrier = pltpu.get_barrier_semaphore()
    pl.semaphore_signal(barrier, inc=1, device_id={"slab": partner})
    greeted = 1
    for step in (-4, -2, 2, 4):
        there = index + step
        inside = jnp.logical_and(there >= 0, there < count)
        greeted = greeted + inside.astype(jnp.int32)

        @pl.when(inside)
        def _():
            pl.semaphore_signal(barrier, inc=1, device_id={"slab": there})

    for fetch in fetches:
        fetch.wait()

    def prepare(slot, real, imag, exact=False):
        for part, w_ref, q_ref in ((0, w_high, q_high), (1, w_low, q_low)):
            if exact and part == 1:
                break
            a = split(real)[part]
            b = split(imag)[part]
            w_ref[slot, :n, :n] = a
            w_ref[slot, :n, n:] = b
            w_ref[slot, n:, :n] = b
            w_ref[slot, n:, n:] = -a
            q_ref[slot, :n] = a.astype(F32).T.astype(BF16)
            q_ref[slot, n:] = b.astype(F32).T.astype(BF16)

    def load(ref, chunk):
        at = slice(chunk * rows, (chunk + 1) * rows)
        high, low = split(ref[at, :])
        r_high[at, :] = high
        r_low[at, :] = low
        high, low = split(ref[at, :].T)
        r_high[n:, at] = high
        r_low[n:, at] = low

    def first(slot, exact=False):
        value = dot(w_high[slot], r_high[...]) + dot(w_high[slot], r_low[...])
        if not exact:
            value += dot(w_low[slot], r_high[...])
        uv[...] = value

    def second(slot, chunk, exact=False):
        total = None
        for side in range(2):
            at = slice(side * n + chunk * rows, side * n + (chunk + 1) * rows)
            high, low = split(uv[at, :])
            k = slice(side * n, (side + 1) * n)
            value = dot(high, q_high[slot, k]) + dot(low, q_high[slot, k])
            if not exact:
                value += dot(high, q_low[slot, k])
            total = value if total is None else total + value
        return total

    def chunk_rows(chunk):
        return slice(chunk * rows, (chunk + 1) * rows)

    def swap(which, source, target):
        return pltpu.make_async_remote_copy(
            src_ref=source,
            dst_ref=target,
            send_sem=swap_send.at[which],
            recv_sem=swap_recv.at[which],
            device_id={"slab": partner},
        )

    def chain_copy(chunk, which):
        return pltpu.make_async_remote_copy(
            src_ref=chain_out.at[pl.ds(chunk * rows, rows)],
            dst_ref=chain_in.at[pl.ds(chunk * rows, rows)],
            send_sem=chain_send.at[which, chunk],
            recv_sem=chain_recv.at[chunk],
            device_id={"slab": (next_far, next_near)[which]},
        )

    def head_copy(which, source, target):
        return pltpu.make_async_remote_copy(
            src_ref=source,
            dst_ref=target,
            send_sem=head_send.at[which],
            recv_sem=head_recv.at[which],
            device_id={"slab": next_near},
        )

    def mid_copy(chunk):
        return pltpu.make_async_remote_copy(
            src_ref=mid_out.at[pl.ds(chunk * rows, rows)],
            dst_ref=mid_in.at[pl.ds(chunk * rows, rows)],
            send_sem=mid_send.at[chunk],
            recv_sem=mid_recv.at[chunk],
            device_id={"slab": partner},
        )

    g_r, g_i = green[0], green[1]
    c_r, c_i = coupling[0], coupling[1]
    maps[0, 0] = dot(g_r, c_r) - dot(g_i, c_i)
    maps[0, 1] = dot(g_r, c_i) + dot(g_i, c_r)
    ct_r = c_r.astype(F32).T.astype(BF16)
    ct_i = c_i.astype(F32).T.astype(BF16)
    maps[1, 0] = dot(ct_r, g_r) + dot(ct_i, g_i)
    maps[1, 1] = dot(ct_r, g_i) - dot(ct_i, g_r)

    pl.semaphore_wait(barrier, greeted)
    swap_map = swap(0, maps.at[1 - core], their_map)
    swap_map.start()

    gamma_row = gamma[...] * occupation[0, 0]

    def source(which):
        real, imag = (
            (maps[1, 0], maps[1, 1])
            if which
            else (green[0].astype(F32), green[1].astype(F32))
        )
        uv[:n] = (real + imag) * gamma_row
        uv[n:] = (imag - real) * gamma_row
        for part, q_ref in ((0, q_high), (1, q_low))[: 1 + which]:
            q_ref[4, :n] = split(real)[part].astype(F32).T.astype(BF16)
            q_ref[4, n:] = split(imag)[part].astype(F32).T.astype(BF16)
        for chunk in range(CHUNKS):
            sources[which, chunk_rows(chunk), :] = second(4, chunk, exact=not which)

    swap_source = swap(1, sources.at[1 - core], their_source)
    for mine in range(2):
        @pl.when(core == mine)
        def _():
            source(1 - mine)
            swap_source.start()
            source(mine)

    def trace_weights():
        f_r, f_i = green[0].astype(F32), green[1].astype(F32)
        trace_w[...] = 0.5 * ((f_i - f_r) + (f_i + f_r).T)

    def own_maps():
        prepare(0, maps[core, 0], maps[core, 1])

        @pl.when(core == 1)
        def _():
            prepare(1, maps[0, 0], maps[0, 1])

        trace_weights()

    def multiply(slot, ref):
        real, imag = split(ref[0]), split(ref[1])
        r_high[:n], r_low[:n] = real
        r_high[n:], r_low[n:] = -imag[0], -imag[1]
        for side in range(2):
            if side == 1:
                r_high[:n], r_low[:n] = imag
                r_high[n:], r_low[n:] = real
            uv[side * n : (side + 1) * n] = (
                dot(w_high[slot, :n], r_high[...])
                + dot(w_high[slot, :n], r_low[...])
                + dot(w_low[slot, :n], r_high[...])
            )

    head_map_copy = head_copy(0, pair_map, head_map)
    head_source_copy = head_copy(1, head_out, head_source)
    sends_map = jnp.logical_and(tail == 0, place > 0)
    swap_map.wait_recv()
    prepare(3, their_map[0], their_map[1])
    own = maps.at[core]
    multiply(3, own)
    pair_map[0] = uv[:n]
    pair_map[1] = uv[n:]

    @pl.when(sends_map)
    def _():
        head_map_copy.start()

    for chunk in range(CHUNKS):
        load(sources.at[core], chunk)
    first(3)
    swap_source.wait_recv()
    for chunk in range(CHUNKS):
        at = chunk_rows(chunk)
        pair_source[at, :] = second(3, chunk) + their_source[at, :]

    @pl.when(sends_map)
    def _():
        head_out[...] = pair_source[...]
        head_source_copy.start()

    @pl.when(jnp.logical_or(tail == 1, place == 0))
    def _():
        prepare(2, pair_map[0], pair_map[1])

    opens = jnp.logical_and(tail == 0, place == 0)

    @pl.when(jnp.logical_not(opens))
    def _():
        own_maps()

    def flow():
        weight_u = 0.5 * (coupling[0].astype(F32) - coupling[1].astype(F32))
        weight_v = 0.5 * (coupling[0].astype(F32) + coupling[1].astype(F32))
        sums[0] = jnp.sum(uv[:n] * weight_u + uv[n:] * weight_v)

    def back(ref):
        sums[1] = jnp.sum(ref[...] * trace_w[...])

    def emit(ref):
        block = ref[...]
        turned = block.T
        out[0] = 0.5 * (block + turned)
        out[1] = 0.5 * (block - turned)

    def relay(slot, source):
        near_first = jnp.logical_and(place == last - 1, core == 0)
        far_first = jnp.logical_and(place < last, jnp.logical_not(near_first))

        for chunk in range(CHUNKS):
            at = chunk_rows(chunk)
            chain_out[at, :] = second(slot, chunk) + source[at, :]

            @pl.when(far_first)
            def _():
                chain_copy(chunk, 0).start()

            @pl.when(near_first)
            def _():
                chain_copy(chunk, 1).start()

        for chunk in range(CHUNKS):
            @pl.when(far_first)
            def _():
                chain_copy(chunk, 1).start()

            @pl.when(near_first)
            def _():
                chain_copy(chunk, 0).start()

    def receive():
        for chunk in range(CHUNKS):
            chain_copy(chunk, 0).wait_recv()
            load(chain_in, chunk)

    ends = jnp.logical_and(tail == 1, jnp.logical_and(place == last, place > 0))
    base = 2 - 2 * ends.astype(jnp.int32)

    def hand_over(slot, source):
        for chunk in range(CHUNKS):
            at = chunk_rows(chunk)
            mid_out[at, :] = second(slot, chunk) + source[at, :]
            mid_copy(chunk).start()

    def chain():
        @pl.when(tail == 0)
        def _():
            @pl.when(place == 0)
            def _():
                row = lax.broadcasted_iota(jnp.int32, (n, n), 0)
                column = lax.broadcasted_iota(jnp.int32, (n, n), 1)
                level = lead_occ[0] * (1 - core).astype(F32)
                chain_in[...] = jnp.where(row == column, level, 0.0)
                uv[:n] = level * (pair_map[0] + pair_map[1])
                uv[n:] = level * (pair_map[1] - pair_map[0])
                for chunk in range(CHUNKS):
                    at = chunk_rows(chunk)
                    head_out[at, :] = second(2, chunk) + pair_source[at, :]
                head_source_copy.start()
                own_maps()
                for chunk in range(CHUNKS):
                    load(chain_in, chunk)

            @pl.when(place > 0)
            def _():
                receive()

            state_in[...] = chain_in[...]

        @pl.when(tail == 1)
        def _():
            @pl.when(place > 0)
            def _():
                head_map_copy.wait_recv()
                prepare(3, head_map[0], head_map[1])
                multiply(base, head_map)
                prepare(4, uv[:n], uv[n:])

            head_source_copy.wait_recv()
            for chunk in range(CHUNKS):
                load(head_source, chunk)
            first(base)

            @pl.when(place == 0)
            def _():
                relay(2, pair_source)
                state_in[...] = head_source[...]

            @pl.when(place > 0)
            def _():
                for chunk in range(CHUNKS):
                    at = chunk_rows(chunk)
                    quad_source[at, :] = second(base, chunk) + jnp.where(
                        ends, sources[core, at, :], pair_source[at, :]
                    )
                receive()
                first(4)

                @pl.when(jnp.logical_not(ends))
                def _():
                    relay(4, quad_source)

                @pl.when(ends)
                def _():
                    hand_over(4, quad_source)

                first(3)
                for chunk in range(CHUNKS):
                    at = chunk_rows(chunk)
                    state_in[at, :] = second(3, chunk) + head_source[at, :]

            for chunk in range(CHUNKS):
                load(state_in, chunk)

        @pl.when(jnp.logical_or(core == 0, jnp.logical_not(ends)))
        def _():
            first(0)

        @pl.when(jnp.logical_not(ends))
        def _():
            hand_over(0, sources.at[core])

        @pl.when(core == 0)
        def _():
            flow()
            emit(mid_out)

        @pl.when(core == 1)
        def _():
            back(state_in)

    def middle():
        for chunk in range(CHUNKS):
            mid_copy(chunk).wait_recv()

        @pl.when(core == 0)
        def _():
            back(mid_in)

        @pl.when(core == 1)
        def _():
            for chunk in range(CHUNKS):
                load(mid_in, chunk)
            first(1)
            for chunk in range(CHUNKS):
                at = chunk_rows(chunk)
                chain_spare[at, :] = second(1, chunk) + sources[0, at, :]
            flow()
            emit(chain_spare)

    chain_spare = their_source
    early = (place <= quads // 2).astype(jnp.int32)

    def phase(step, carry):
        @pl.when(step + early == 1)
        def _():
            chain()

        @pl.when(step + early != 1)
        def _():
            middle()

        return carry

    lax.fori_loop(0, 2, phase, 0)
    current[0] = energy_weight[0] * (sums[0] - sums[1]) / n

    swap_map.wait_send()
    swap_source.wait_send()
    for chunk in range(CHUNKS):
        mid_copy(chunk).wait_send()

    @pl.when(tail == 0)
    def _():
        head_source_copy.wait_send()

        @pl.when(place > 0)
        def _():
            head_map_copy.wait_send()

    @pl.when(jnp.logical_and(tail == 1, place < last))
    def _():
        for which in range(2):
            for chunk in range(CHUNKS):
                chain_copy(chunk, which).wait_send()


def on_device(green, couplings, gamma, occupation, lead_occ, energy_weight):
    n = green.shape[-1]
    vmem = pl.BlockSpec(memory_space=pltpu.VMEM)
    hbm = pl.BlockSpec(memory_space=pl.ANY)
    smem = pl.BlockSpec(memory_space=pltpu.SMEM)
    block = lambda *lead: pltpu.VMEM((*lead, n, n), F32)
    wide = lambda *shape: pltpu.VMEM(shape, BF16)
    state, current = pl.pallas_call(
        kernel,
        out_shape=(
            jax.ShapeDtypeStruct((2, n, n), F32),
            jax.ShapeDtypeStruct((1,), F32),
        ),
        in_specs=[hbm, hbm, hbm, smem, smem, smem],
        out_specs=(vmem, smem),
        scratch_shapes=[
            wide(2, n, n),
            wide(2, n, n),
            pltpu.VMEM((1, n), F32),
            pltpu.SemaphoreType.DMA((3,)),
            block(2, 2),
            block(2),
            block(2),
            block(),
            wide(5, 2 * n, 2 * n),
            wide(5, 2 * n, 2 * n),
            wide(5, 2 * n, n),
            wide(5, 2 * n, n),
            wide(2 * n, n),
            wide(2 * n, n),
            pltpu.VMEM((2 * n, n), F32),
            block(2),
            block(),
            block(),
            block(2),
            block(),
            block(),
            block(),
            block(),
            block(),
            block(),
            block(),
            block(),
            pltpu.SMEM((2,), F32),
            pltpu.SemaphoreType.DMA((2,)),
            pltpu.SemaphoreType.DMA((2,)),
            pltpu.SemaphoreType.DMA((2,)),
            pltpu.SemaphoreType.DMA((2,)),
            pltpu.SemaphoreType.DMA((2, CHUNKS)),
            pltpu.SemaphoreType.DMA((CHUNKS,)),
            pltpu.SemaphoreType.DMA((CHUNKS,)),
            pltpu.SemaphoreType.DMA((CHUNKS,)),
        ],
        compiler_params=pltpu.CompilerParams(
            collective_id=0, has_side_effects=True, vmem_limit_bytes=62 * 2**20
        ),
    )(
        green.reshape(2, n, n),
        couplings.reshape(2, n, n),
        gamma,
        occupation,
        lead_occ,
        energy_weight,
    )
    return state.reshape(1, 1, 2, n, n), current


def solution(mesh):
    return jax.shard_map(
        on_device,
        mesh=mesh,
        in_specs=(
            P("group", "slab", None, None, None),
            P("slab", None, None, None),
            P("slab", None),
            P("group", "slab"),
            P("group"),
            P("group"),
        ),
        out_specs=(P("group", "slab", None, None, None), P(("group", "slab"))),
        check_vma=False,
    )
```
